256 devices in a mesh: factor: 8 (over z_lo, core), dp: 32 (over z_hi, y, x).
Axes of the slice: x: 4, y: 4, z: 8 (z_hi: 2, z_lo: 4; z = z_hi * 4 + z_lo), core: 2. Of those that a mesh axis runs over, the one named last changes fastest.
Arguments:
- acts: bfloat16 [2, 65536, 4096], P(None, ('factor', 'dp'))
- grads_out: bfloat16 [2, 65536, 4096], P(None, ('factor', 'dp'))
- grad: bfloat16 [2, 4096, 4096], P(None, 'dp', 'factor'), may hold values from -0.59765625 to 0.59765625
- bases_a: float32 [16, 4096, 128], P('factor', 'dp'), may hold values from -0.5 to 0.5
- bases_g: float32 [16, 4096, 128], P('factor', 'dp'), may hold values from -0.5 to 0.5
- owner_slot: int32 [2], replicated, may hold values from 0 to 15, as said below
Outputs:
- update: bfloat16 [2, 4096, 4096], P(None, 'dp', 'factor')
The draws below stay inside these ranges and needn't reach their ends.
Inputs may be any that keep to these rules, and one draw needn't show every extreme that they name: The values are distinct and one layer always uses the last slot; layer l belongs to owner group owner_slot[l] // 2 (the index along factor) and uses its slot owner_slot[l] % 2.
All inputs are finite; a program needn't handle non-finite values.
Results may differ from the reference program's by a relative error of at most 0.001.
Values may be sent and summed in bfloat16 or wider, within the bound.
A program may use at most 128 MiB of HBM per device.

```python
import math
import jax
import jax.numpy as jnp
from jax import lax

D = 4096
BLOCK = 128
BLOCKS = 32
LAYERS = 2
ROWS_DEV = 256
TOKENS = 65536
SLOTS_ALL = 16
N_DP = 32


def shaped_rows(key, base_values):
    key_row, key_col = jax.random.split(key, 2)
    row_scale = jnp.exp(jax.random.uniform(key_row, (LAYERS, TOKENS, 1), jnp.float32, math.log(0.1), 0.0))
    position = jnp.arange(TOKENS, dtype=jnp.float32).reshape(1, TOKENS, 1)
    row_scale = row_scale * (1.0 + 2.0 * position / max(TOKENS - 1, 1))
    col_scale = jnp.exp(jax.random.uniform(key_col, (LAYERS, 1, D), jnp.float32, math.log(0.3), math.log(3.0)))
    device_block = jnp.arange(TOKENS, dtype=jnp.int32) // ROWS_DEV % BLOCKS
    column_block = jnp.arange(D, dtype=jnp.int32) // BLOCK
    boost = jnp.where(device_block[:, None] == column_block[None, :], 4.0, 1.0).astype(jnp.float32)
    return base_values * row_scale * col_scale * boost[None, :, :]


def draw_acts(key, part):
    key = jax.random.fold_in(key, 11)
    key_base, key_rest = jax.random.split(key)
    base_values = jax.random.normal(key_base, (LAYERS, TOKENS, D), jnp.float32)
    return shaped_rows(key_rest, base_values).astype(jnp.bfloat16)


def draw_grads_out(key, part):
    key = jax.random.fold_in(key, 23)
    key_base, key_rest = jax.random.split(key)
    base_values = jax.random.normal(key_base, (LAYERS, TOKENS, D), jnp.float32)
    return shaped_rows(key_rest, base_values).astype(jnp.bfloat16)


def draw_owner_slot(key, part):
    key = jax.random.fold_in(key, 37)
    key_order, key_place = jax.random.split(key)
    shuffled = jax.random.permutation(key_order, SLOTS_ALL - 1)[:LAYERS].astype(jnp.int32)
    chosen = jax.random.randint(key_place, (), 0, LAYERS, jnp.int32)
    places = jnp.arange(LAYERS, dtype=jnp.int32)
    return jnp.where(places == chosen, jnp.int32(SLOTS_ALL - 1), shuffled).astype(jnp.int32)


def block_scale(stream_key, extent, pieces, least, largest):
    factor_of = 1.0
    for dim, parts in pieces:
        draws = jax.random.uniform(jax.random.fold_in(jax.random.fold_in(stream_key, 6), dim), (parts,), jnp.float32, least / len(pieces), largest / len(pieces))
        factor_of = factor_of * jnp.repeat(jnp.exp(draws), extent[dim] // parts).reshape((-1,) + (1,) * (len(extent) - 1 - dim))
    return factor_of


def scatter_about(key, extent, scale, most, shards=(), kind=jnp.bfloat16):
    array = scale * jax.random.normal(key, extent, jnp.float32)
    if shards:
        array = array * block_scale(key, extent, shards, -0.22, 0.18)
    return jnp.clip(array, -most, most).astype(kind)


def setup_inputs(seed: int = 0) -> dict:
    keys = jax.random.split(jax.random.key(seed), 7)
    return {
        "acts": draw_acts(jax.random.fold_in(keys[6], 71), 0),
        "grads_out": draw_grads_out(jax.random.fold_in(keys[6], 71), 0),
        "grad": scatter_about(keys[2], (LAYERS, D, D), 0.1, 0.59765625, ((1, 32), (2, 8))),
        "bases_a": scatter_about(keys[3], (SLOTS_ALL, D, BLOCK), BLOCK ** -0.5, 0.5, ((0, 8), (1, 32)), jnp.float32),
        "bases_g": scatter_about(keys[4], (SLOTS_ALL, D, BLOCK), BLOCK ** -0.5, 0.5, ((0, 8), (1, 32)), jnp.float32),
        "owner_slot": draw_owner_slot(jax.random.fold_in(keys[6], 71), 0),
    }


damping = 0.05


def block_factor(values):
    grouped = values.reshape(-1, ROWS_DEV * N_DP, BLOCKS, BLOCK)

    def accumulate(running, block_rows):
        cast_rows = block_rows.astype(jnp.float32)
        return running + jnp.einsum('rnb,rnc->nbc', cast_rows, cast_rows), None

    running, unused = lax.scan(accumulate, jnp.zeros((BLOCKS, BLOCK, BLOCK), jnp.float32), grouped)
    return running / TOKENS


def eigen_scale(factor_blocks, basis):
    turned = jnp.einsum('nbc,ncd->nbd', factor_blocks, basis, precision=lax.Precision.HIGHEST)
    return jnp.sum(basis * turned, axis=1)


def precondition(gradient, basis_left, basis_right, scale_left, scale_right):
    left_count = basis_left.shape[0]
    right_count = basis_right.shape[0]
    values = gradient.astype(jnp.float32).reshape(left_count, BLOCK, right_count, BLOCK)
    rotated = jnp.einsum('ibc,ibjd->icjd', basis_left, values, precision=lax.Precision.HIGHEST)
    inner = jnp.einsum('icjd,jde->icje', rotated, basis_right, precision=lax.Precision.HIGHEST)
    scaled = inner / (scale_left[:, :, None, None] * scale_right[None, None, :, :] + damping)
    restored = jnp.einsum('icje,jfe->icjf', scaled, basis_right, precision=lax.Precision.HIGHEST)
    result = jnp.einsum('iac,icjf->iajf', basis_left, restored, precision=lax.Precision.HIGHEST)
    return result.reshape(left_count * BLOCK, right_count * BLOCK).astype(jnp.bfloat16)


def reference(acts, grads_out, grad, bases_a, bases_g, owner_slot):
    results = []
    for position in range(LAYERS):
        slot_index = owner_slot[position].astype(jnp.int32)
        basis_left = lax.dynamic_index_in_dim(bases_a, slot_index, 0, keepdims=False).reshape(BLOCKS, BLOCK, BLOCK)
        basis_right = lax.dynamic_index_in_dim(bases_g, slot_index, 0, keepdims=False).reshape(BLOCKS, BLOCK, BLOCK)
        scale_left = eigen_scale(block_factor(acts[position]), basis_left)
        scale_right = eigen_scale(block_factor(grads_out[position]), basis_right)
        results.append(precondition(grad[position], basis_left, basis_right, scale_left, scale_right))
    return jnp.stack(results)
```

```python
import functools

import jax
import jax.numpy as jnp
from jax import lax
from jax.experimental import pallas as pl
from jax.experimental.pallas import tpu as pltpu
from jax.sharding import PartitionSpec as P

MESH = pl.DeviceIdType.MESH
B = 128
SLOTS = 2
DAMPING = 0.05
HIGHEST = lax.Precision.HIGHEST
F32 = jnp.float32

CHUNK = 8 * B + 8
PIECE = 2 * B + 8
ORDER = (2, 1, 3, 0)


def dot(a, b, ca, cb, precision=None):
    return lax.dot_general(a, b, (((ca,), (cb,)), ((), ())), precision=precision, preferred_element_type=F32)


def kernel(total_rows, slot_ref, acts, grads, grad, bases_a, bases_g, out,
           xs, gs, bs, part, core_in, own, in1, two, in2, qc, qc_in, qs, qs_in, qm, qbuf, qa, qg,
           zs, zr, sa, sg, keep, inner_s,
           ld, s_core, r_core, s_one, r_one, s_two, r_two, s_q, r_q, s_rs, r_rs, s_ag, r_ag,
           s_qy, r_qy, s_qx, r_qx, s_z, r_z, s_xy, r_xy, s_p, r_p):
    f = lax.axis_index("factor")
    d = lax.axis_index("dp")
    z_lo, c = f // 2, f % 2
    z_hi, y, x = d // 16, (d // 4) % 4, d % 4
    z = 4 * z_hi + z_lo
    row_col = 4 * y + x
    other = 1 - c
    first, second = x + c * (y - x), y + c * (x - y)
    first_other = x + other * (y - x)
    side = 1 - (y + c) % 2
    source_row = 2 * (z_lo % 2) + c
    is_source = y == source_row
    half_here = z_lo // 2

    def at(zz, yy, xx, cc):
        return (2 * (zz % 4) + cc, 16 * (zz // 4) + 4 * yy + xx)

    def ring(t, u):
        return at(z, u + c * (t - u), t + c * (u - t), c)

    def remote(src, dst, send, recv, to):
        return pltpu.make_async_remote_copy(src_ref=src, dst_ref=dst, send_sem=send, recv_sem=recv,
                                            device_id=to, device_id_type=MESH)

    partner = at(z, y, x, other)

    loads = [
        pltpu.make_async_copy(bases_a, bs.at[0], ld.at[0]),
        pltpu.make_async_copy(bases_g, bs.at[1], ld.at[1]),
        pltpu.make_async_copy(acts, xs.at[0], ld.at[2]),
        pltpu.make_async_copy(grads, xs.at[1], ld.at[3]),
        pltpu.make_async_copy(grad, gs, ld.at[4]),
    ]
    for copy in loads:
        copy.start()

    barrier = pltpu.get_barrier_semaphore()

    def signal(to):
        pl.semaphore_signal(barrier, inc=1, device_id=to, device_id_type=MESH)

    signal(partner)
    for k in range(1, 16):
        n = (row_col + k) % 16
        signal(at(z, n // 4, n % 4, c))
    for k in range(1, 8):
        signal(at((z + k) % 8, y, x, c))

    loads[0].wait()
    loads[1].wait()
    for l in range(2):
        slot = slot_ref[l]
        mine = (slot // SLOTS) == f
        for which, sd in ((0, side), (1, 1 - side)):
            picked = jnp.where(slot % SLOTS == 0, bs[sd, 0], bs[sd, 1])
            qc[which, l] = jnp.where(mine, picked, jnp.zeros_like(picked))
    pl.semaphore_wait(barrier, 23)

    core_q = remote(qc.at[1], qc_in, s_q, r_q, partner)
    core_q.start()

    iota_r = lax.broadcasted_iota(jnp.int32, (B, B), 0)
    iota_c = lax.broadcasted_iota(jnp.int32, (B, B), 1)
    upper = iota_r <= iota_c
    on_diag = iota_r == iota_c

    def chunk_terms(core, t, dst, add):
        def one(m, carry):
            u, h = m // 2, m % 2
            xb, yb = t + core * (u - t), u + core * (t - u)
            col = pl.multiple_of((16 * h + 4 * yb + xb) * B, B)
            sd = 1 - (yb + core) % 2
            x0 = xs[sd, 0, :, pl.ds(col, B)]
            x1 = xs[sd, 1, :, pl.ds(col, B)]
            f0 = dot(x0, x0, 0, 0)
            f1 = dot(x1, x1, 0, 0)
            packed = jnp.where(upper, f0, f1)
            diag = jnp.sum(jnp.where(on_diag, f1, 0.0), axis=0, keepdims=True)
            rows = pl.ds(pl.multiple_of(m * B, B), B)
            row = pl.ds(8 * B + m, 1)
            if add is not None:
                packed = packed + add[rows, :]
                diag = diag + add[row, :]
            dst[rows, :] = packed
            dst[row, :] = diag
            return carry

        lax.fori_loop(0, 8, one, 0)

    loads[2].wait()
    loads[3].wait()

    core_copies, one_copies = [], []

    def for_partner(k):
        chunk_terms(other, (first_other + ORDER[k]) % 4, part.at[k], None)
        copy = remote(part.at[k], core_in.at[k], s_core.at[k], r_core.at[k], partner)
        copy.start()
        core_copies.append(copy)

    def for_ring(k):
        core_copies[k].wait_recv()
        t = (first + ORDER[k]) % 4
        chunk_terms(c, t, own.at[k], core_in.at[k])
        if k < 3:
            copy = remote(own.at[k], in1.at[k], s_one.at[k], r_one.at[k], ring(t, second))
            copy.start()
            one_copies.append(copy)

    for_partner(0)

    core_q.wait_recv()
    for l in range(2):
        qs[l] = qc[0, l] + qc_in[l]
    rs_copies = []
    for k in range(1, 4):
        zz = (z_lo + k) % 4
        copy = remote(qs.at[:, pl.ds(pl.multiple_of(32 * zz, 32), 32), :], qs_in.at[k - 1],
                      s_rs.at[k - 1], r_rs.at[k - 1], at(4 * z_hi + zz, y, x, c))
        copy.start()
        rs_copies.append(copy)

    for_partner(1)
    for_ring(0)

    for copy in rs_copies:
        copy.wait_recv()
    here = pl.ds(pl.multiple_of(32 * z_lo, 32), 32)
    summed = qs[:, here, :] + qs_in[0] + qs_in[1] + qs_in[2]
    qm[...] = summed
    qbuf[z_hi, :, here, :] = summed
    ag_copies = []
    for k in range(1, 8):
        copy = remote(qm, qbuf.at[z_hi, :, here, :], s_ag.at[k - 1], r_ag.at[k - 1], at((z + k) % 8, y, x, c))
        copy.start()
        ag_copies.append(copy)

    for_partner(2)
    for_ring(1)
    for_partner(3)
    for_ring(2)
    for_ring(3)

    for k in range(1, 8):
        zz = (z + 8 - k) % 8
        rows = pl.ds(pl.multiple_of(32 * (zz % 4), 32), 32)
        remote(qm, qbuf.at[zz // 4, :, rows, :], s_ag.at[k - 1], r_ag.at[k - 1], partner).wait_recv()

    qy_copies = []
    for k in range(1, 4):
        copy = remote(qbuf.at[half_here], qg.at[x], s_qy.at[k - 1], r_qy, at(z, (y + k) % 4, x, c))
        qy_copies.append(copy)
    qa_copy = remote(qbuf.at[z_hi], qa, s_p.at[0], r_p.at[0], partner)

    @pl.when(is_source)
    def _():
        for copy in qy_copies:
            copy.start()
        qg[x] = qbuf[half_here]

    @pl.when(side == 0)
    def _():
        qa_copy.start()
        qa[...] = qbuf[z_hi]

    for copy in one_copies:
        copy.wait_recv()
    diags = slice(8 * B, CHUNK)
    diag_sum = own[3, diags, :] + in1[0, diags, :] + in1[1, diags, :] + in1[2, diags, :]
    two_copies = []
    for k in range(4):
        u = (second + ORDER[k]) % 4
        rows = pl.ds(pl.multiple_of(2 * B * u, 2 * B), 2 * B)
        two[k, : 2 * B, :] = own[3, rows, :] + in1[0, rows, :] + in1[1, rows, :] + in1[2, rows, :]
        two[k, 2 * B :, :] = diag_sum
        if k < 3:
            copy = remote(two.at[k], in2.at[k], s_two.at[k], r_two.at[k], ring(first, u))
            copy.start()
            two_copies.append(copy)

    @pl.when(jnp.logical_not(is_source))
    def _():
        qy_copies[0].wait_recv()

    qx_copies = []
    for k in range(1, 4):
        copy = remote(qg.at[x], qg.at[x], s_qx.at[k - 1], r_qx.at[k - 1], at(z, y, (x + k) % 4, c))
        copy.start()
        qx_copies.append(copy)

    for copy in two_copies:
        copy.wait_recv()

    zs[...] = jnp.zeros_like(zs)
    for h in range(2):
        rows = slice(h * B, (h + 1) * B)
        packed = two[3, rows, :] + in2[0, rows, :] + in2[1, rows, :] + in2[2, rows, :]
        row = pl.ds(2 * B + 2 * second + h, 1)
        diag = two[3, row, :] + in2[0, row, :] + in2[1, row, :] + in2[2, row, :]
        m0 = jnp.where(upper, jnp.where(on_diag, packed, 2.0 * packed), 0.0)
        m1 = jnp.where(upper, jnp.where(on_diag, jnp.broadcast_to(diag, (B, B)), 0.0), 2.0 * packed)
        for l, m in ((0, m0), (1, m1)):
            q = qbuf[h, l]
            zs[2 * h + l : 2 * h + l + 1, :] = jnp.sum(q * dot(m, q, 1, 0, HIGHEST), axis=0, keepdims=True)
    z_copies = []
    for k in range(1, 8):
        copy = remote(zs, zr.at[k], s_z.at[k - 1], r_z.at[k - 1], at((z + k) % 8, y, x, c))
        copy.start()
        z_copies.append(copy)
    zr[0] = zs[...]

    @pl.when(side == 1)
    def _():
        qa_copy.wait_recv()

    for k in range(1, 4):
        from_x = (x + 4 - k) % 4
        remote(qg.at[x], qg.at[from_x], s_qx.at[k - 1], r_qx.at[k - 1], partner).wait_recv()
    loads[4].wait()
    for l in range(2):
        rotated = dot(qa[l], gs[l].astype(F32), 0, 0, HIGHEST)
        for q in range(4):
            inner_s[l, :, q * B : (q + 1) * B] = dot(rotated[:, q * B : (q + 1) * B], qg[q, l], 1, 0, HIGHEST)

    for copy in z_copies:
        copy.wait_recv()
    scales = zr[0]
    for k in range(1, 8):
        scales = scales + zr[k]
    scales = scales / total_rows
    keep[...] = scales

    xy_copies = []
    for k in range(1, 16):
        n = (row_col + k) % 16
        xy_copies.append(remote(zs, sg.at[x], s_xy.at[k - 1], r_xy.at[x], at(z, n // 4, n % 4, c)))
    sa_copy = remote(zs, sa, s_p.at[1], r_p.at[1], partner)

    for copy in z_copies:
        copy.wait_send()

    @pl.when(is_source)
    def _():
        zs[:2, :] = keep[pl.ds(2 * half_here, 2), :]
        for copy in xy_copies:
            copy.start()
        sg[x] = zs[...]

    @pl.when(side == 0)
    def _():
        zs[:2, :] = keep[pl.ds(2 * z_hi, 2), :]
        sa_copy.start()
        sa[...] = zs[...]

    @pl.when(side == 1)
    def _():
        sa_copy.wait_recv()

    for q in range(4):
        @pl.when(jnp.logical_not(jnp.logical_and(is_source, x == q)))
        def _():
            remote(zs, sg.at[q], s_xy.at[0], r_xy.at[q], partner).wait_recv()

    for l in range(2):
        left = jnp.transpose(jnp.broadcast_to(sa[l : l + 1, :], (B, B)))
        for q in range(4):
            cols = slice(q * B, (q + 1) * B)
            scaled = inner_s[l, :, cols] / (left * sg[q, l : l + 1, :] + DAMPING)
            inner_s[l, :, cols] = dot(scaled, qg[q, l], 1, 1, HIGHEST)
        out[l] = dot(qa[l], inner_s[l], 1, 0, HIGHEST).astype(out.dtype)

    for copy in [core_q] + core_copies + one_copies + rs_copies + ag_copies + two_copies + qx_copies:
        copy.wait_send()

    @pl.when(is_source)
    def _():
        for copy in qy_copies + xy_copies:
            copy.wait_send()

    @pl.when(side == 0)
    def _():
        qa_copy.wait_send()
        sa_copy.wait_send()


def body(acts, grads_out, grad, bases_a, bases_g, owner_slot):
    rows = acts.shape[1]
    total_rows = rows * lax.axis_size("dp") * lax.axis_size("factor")
    dma = pltpu.SemaphoreType.DMA
    scratch = [
        pltpu.VMEM((2,) + acts.shape, acts.dtype),
        pltpu.VMEM(grad.shape, grad.dtype),
        pltpu.VMEM((2,) + bases_a.shape, F32),
        pltpu.VMEM((4, CHUNK, B), F32),
        pltpu.VMEM((4, CHUNK, B), F32),
        pltpu.VMEM((4, CHUNK, B), F32),
        pltpu.VMEM((3, CHUNK, B), F32),
        pltpu.VMEM((4, PIECE, B), F32),
        pltpu.VMEM((3, PIECE, B), F32),
        pltpu.VMEM((2, 2, B, B), F32),
        pltpu.VMEM((2, B, B), F32),
        pltpu.VMEM((2, B, B), F32),
        pltpu.VMEM((3, 2, 32, B), F32),
        pltpu.VMEM((2, 32, B), F32),
        pltpu.VMEM((2, 2, B, B), F32),
        pltpu.VMEM((2, B, B), F32),
        pltpu.VMEM((4, 2, B, B), F32),
        pltpu.VMEM((8, B), F32),
        pltpu.VMEM((8, 8, B), F32),
        pltpu.VMEM((8, B), F32),
        pltpu.VMEM((4, 8, B), F32),
        pltpu.VMEM((8, B), F32),
        pltpu.VMEM((2, B, 4 * B), F32),
        dma((5,)),
        dma((4,)), dma((4,)),
        dma((3,)), dma((3,)),
        dma((3,)), dma((3,)),
        dma, dma,
        dma((3,)), dma((3,)),
        dma((7,)), dma((7,)),
        dma((3,)), dma,
        dma((3,)), dma((3,)),
        dma((7,)), dma((7,)),
        dma((15,)), dma((4,)),
        dma((2,)), dma((2,)),
    ]
    hbm = pl.BlockSpec(memory_space=pl.ANY)
    return pl.pallas_call(
        functools.partial(kernel, total_rows),
        out_shape=jax.ShapeDtypeStruct(grad.shape, jnp.bfloat16),
        in_specs=[pl.BlockSpec(memory_space=pltpu.SMEM)] + [hbm] * 5,
        out_specs=pl.BlockSpec(memory_space=pltpu.VMEM),
        scratch_shapes=scratch,
        compiler_params=pltpu.CompilerParams(
            collective_id=0, has_side_effects=True, vmem_limit_bytes=48 * 1024 * 1024
        ),
        cost_estimate=pl.CostEstimate(flops=2 * 10**9, bytes_accessed=10**7, transcendentals=0),
    )(owner_slot, acts, grads_out, grad, bases_a, bases_g)


def solution(mesh):
    tokens = P(None, ("factor", "dp"), None)
    bases = P("factor", "dp", None)
    split = P(None, "dp", "factor")
    in_specs = (tokens, tokens, split, bases, bases, P())
    return jax.shard_map(body, mesh=mesh, in_specs=in_specs, out_specs=split, check_vma=False)
```

```python
import functools

import jax
import jax.numpy as jnp
from jax import lax
from jax.experimental import pallas as pl
from jax.experimental.pallas import tpu as pltpu
from jax.sharding import PartitionSpec as P

MESH = pl.DeviceIdType.MESH
B = 128
SLOTS = 2
DAMPING = 0.05
HIGHEST = lax.Precision.HIGHEST
F32 = jnp.float32

CHUNK = 8 * B + 8
PIECE = 2 * B + 8
SIDE = 24
FULL = 32500.0
TINY = 1e-37
ORDER = (2, 1, 3, 0)


def dot(a, b, ca, cb, precision=None):
    return lax.dot_general(a, b, (((ca,), (cb,)), ((), ())), precision=precision, preferred_element_type=F32)


def kernel(total_rows, slot_ref, acts, grads, grad, bases_a, bases_g, out,
           xs, gs, bs, part, core_in, own, code, norm, in_code, in_norm, two, in2, qc, qc_in, qs, qs_in, qm, qbuf, qa, qg,
           zs, zr, sa, sg, keep, rot, inner_s,
           ld, s_core, r_core, s_one, r_one, s_norm, r_norm, s_two, r_two, s_q, r_q, s_rs, r_rs, s_ag, r_ag,
           s_qy, r_qy, s_qx, r_qx, s_z, r_z, s_xy, r_xy, s_p, r_p):
    f = lax.axis_index("factor")
    d = lax.axis_index("dp")
    z_lo, c = f // 2, f % 2
    z_hi, y, x = d // 16, (d // 4) % 4, d % 4
    z = 4 * z_hi + z_lo
    row_col = 4 * y + x
    other = 1 - c
    first, second = x + c * (y - x), y + c * (x - y)
    first_other = x + other * (y - x)
    side = 1 - (y + c) % 2
    source_row = 2 * (z_lo % 2) + c
    is_source = y == source_row
    half_here = z_lo // 2

    def at(zz, yy, xx, cc):
        return (2 * (zz % 4) + cc, 16 * (zz // 4) + 4 * yy + xx)

    def ring(t, u):
        return at(z, u + c * (t - u), t + c * (u - t), c)

    def remote(src, dst, send, recv, to):
        return pltpu.make_async_remote_copy(src_ref=src, dst_ref=dst, send_sem=send, recv_sem=recv,
                                            device_id=to, device_id_type=MESH)

    partner = at(z, y, x, other)

    loads = [
        pltpu.make_async_copy(bases_a, bs.at[0], ld.at[0]),
        pltpu.make_async_copy(bases_g, bs.at[1], ld.at[1]),
        pltpu.make_async_copy(acts, xs.at[0], ld.at[2]),
        pltpu.make_async_copy(grads, xs.at[1], ld.at[3]),
        pltpu.make_async_copy(grad, gs, ld.at[4]),
    ]
    for copy in loads:
        copy.start()

    barrier = pltpu.get_barrier_semaphore()

    def signal(to):
        pl.semaphore_signal(barrier, inc=1, device_id=to, device_id_type=MESH)

    signal(partner)
    for k in range(1, 16):
        n = (row_col + k) % 16
        signal(at(z, n // 4, n % 4, c))
    for k in range(1, 8):
        signal(at((z + k) % 8, y, x, c))

    loads[0].wait()
    loads[1].wait()
    for l in range(2):
        slot = slot_ref[l]
        mine = (slot // SLOTS) == f
        for which, sd in ((0, side), (1, 1 - side)):
            picked = jnp.where(slot % SLOTS == 0, bs[sd, 0], bs[sd, 1])
            qc[which, l] = jnp.where(mine, picked, jnp.zeros_like(picked))
    pl.semaphore_wait(barrier, 23)

    core_q = remote(qc.at[1], qc_in, s_q, r_q, partner)
    core_q.start()

    iota_r = lax.broadcasted_iota(jnp.int32, (B, B), 0)
    iota_c = lax.broadcasted_iota(jnp.int32, (B, B), 1)
    upper = iota_r <= iota_c
    on_diag = iota_r == iota_c

    iota_16 = lax.broadcasted_iota(jnp.int32, (16, B), 0)

    def norms_of(tile, m):
        def outer(row):
            return dot(jnp.where(iota_16 == row, tile, 0.0).astype(jnp.bfloat16), tile.astype(jnp.bfloat16), 0, 0)

        return jnp.where(upper, outer(m), outer(8 + m))

    def encode(k):
        diag0 = [jnp.sum(jnp.where(on_diag, own[k, m * B : (m + 1) * B, :], 0.0), axis=0, keepdims=True)
                 for m in range(8)]
        diag1 = own[k, 8 * B :, :]
        diag = jnp.concatenate(diag0 + [diag1], axis=0)
        inverse = jnp.where(diag > TINY, lax.rsqrt(jnp.maximum(diag, TINY)), 1.0)
        tile = inverse.astype(jnp.bfloat16).astype(F32)
        norm[k, :16, :] = tile
        norm[k, 16:, :] = diag1
        for m in range(8):
            rows = slice(m * B, (m + 1) * B)
            unit = own[k, rows, :] * norms_of(tile, m)
            code[k, rows, :] = jnp.round(unit * FULL).astype(jnp.int32).astype(jnp.int16)

    def chunk_terms(core, t, dst, add):
        def one(m, carry):
            u, h = m // 2, m % 2
            xb, yb = t + core * (u - t), u + core * (t - u)
            col = pl.multiple_of((16 * h + 4 * yb + xb) * B, B)
            sd = 1 - (yb + core) % 2
            x0 = xs[sd, 0, :, pl.ds(col, B)]
            x1 = xs[sd, 1, :, pl.ds(col, B)]
            f0 = dot(x0, x0, 0, 0)
            f1 = dot(x1, x1, 0, 0)
            packed = jnp.where(upper, f0, f1)
            diag = jnp.sum(jnp.where(on_diag, f1, 0.0), axis=0, keepdims=True)
            rows = pl.ds(pl.multiple_of(m * B, B), B)
            row = pl.ds(8 * B + m, 1)
            if add is not None:
                packed = packed + add[rows, :]
                diag = diag + add[row, :]
            dst[rows, :] = packed
            dst[row, :] = diag
            return carry

        lax.fori_loop(0, 8, one, 0, unroll=True)

    core_copies, one_copies = [], []

    def for_partner(k):
        chunk_terms(other, (first_other + ORDER[k]) % 4, part.at[k], None)
        copy = remote(part.at[k], core_in.at[k], s_core.at[k], r_core.at[k], partner)
        copy.start()
        core_copies.append(copy)

    def for_ring(k):
        core_copies[k].wait_recv()
        t = (first + ORDER[k]) % 4
        chunk_terms(c, t, own.at[k], core_in.at[k])
        if k < 3:
            encode(k)
            to = ring(t, second)
            for copy in (remote(norm.at[k], in_norm.at[k], s_norm.at[k], r_norm.at[k], to),
                         remote(code.at[k], in_code.at[k], s_one.at[k], r_one.at[k], to)):
                copy.start()
                one_copies.append(copy)

    core_q.wait_recv()
    for l in range(2):
        qs[l] = qc[0, l] + qc_in[l]
    rs_copies = []
    for k in range(1, 4):
        zz = (z_lo + k) % 4
        copy = remote(qs.at[:, pl.ds(pl.multiple_of(32 * zz, 32), 32), :], qs_in.at[k - 1],
                      s_rs.at[k - 1], r_rs.at[k - 1], at(4 * z_hi + zz, y, x, c))
        copy.start()
        rs_copies.append(copy)

    loads[2].wait()
    loads[3].wait()
    for k in range(4):
        for_partner(k)
    for_ring(0)
    for_ring(1)

    for copy in rs_copies:
        copy.wait_recv()
    here = pl.ds(pl.multiple_of(32 * z_lo, 32), 32)
    summed = qs[:, here, :] + qs_in[0] + qs_in[1] + qs_in[2]
    qm[...] = summed
    qbuf[z_hi, :, here, :] = summed
    ag_copies = []
    for k in range(1, 8):
        copy = remote(qm, qbuf.at[z_hi, :, here, :], s_ag.at[k - 1], r_ag.at[k - 1], at((z + k) % 8, y, x, c))
        copy.start()
        ag_copies.append(copy)

    for_ring(2)
    for_ring(3)

    for k in range(1, 8):
        zz = (z + 8 - k) % 8
        rows = pl.ds(pl.multiple_of(32 * (zz % 4), 32), 32)
        remote(qm, qbuf.at[zz // 4, :, rows, :], s_ag.at[k - 1], r_ag.at[k - 1], partner).wait_recv()

    qy_copies = []
    for k in range(1, 4):
        copy = remote(qbuf.at[half_here], qg.at[x], s_qy.at[k - 1], r_qy, at(z, (y + k) % 4, x, c))
        qy_copies.append(copy)
    qa_copy = remote(qbuf.at[z_hi], qa, s_p.at[0], r_p.at[0], partner)

    @pl.when(is_source)
    def _():
        for copy in qy_copies:
            copy.start()
        qg[x] = qbuf[half_here]

    @pl.when(side == 0)
    def _():
        qa_copy.start()
        qa[...] = qbuf[z_hi]

    for copy in one_copies:
        copy.wait_recv()
    diag_sum = own[3, 8 * B :, :] + in_norm[0, 16:, :] + in_norm[1, 16:, :] + in_norm[2, 16:, :]
    tiles = [in_norm[i, :16, :] for i in range(3)]
    two_copies = []
    for k in range(4):
        u = (second + ORDER[k]) % 4
        for h in range(2):
            m = 2 * u + h
            rows = pl.ds(pl.multiple_of(B * m, B), B)
            total = own[3, rows, :]
            for i in range(3):
                unit = in_code[i, rows, :].astype(jnp.int32).astype(F32) * (1.0 / FULL)
                total = total + unit / norms_of(tiles[i], m)
            two[k, h * B : (h + 1) * B, :] = total
        two[k, 2 * B :, :] = diag_sum
        if k < 3:
            copy = remote(two.at[k], in2.at[k], s_two.at[k], r_two.at[k], ring(first, u))
            copy.start()
            two_copies.append(copy)

    @pl.when(jnp.logical_not(is_source))
    def _():
        qy_copies[0].wait_recv()

    qx_copies = []
    for k in range(1, 4):
        copy = remote(qg.at[x], qg.at[x], s_qx.at[k - 1], r_qx.at[k - 1], at(z, y, (x + k) % 4, c))
        copy.start()
        qx_copies.append(copy)

    for copy in two_copies:
        copy.wait_recv()

    zs[...] = jnp.zeros_like(zs)
    for h in range(2):
        rows = slice(h * B, (h + 1) * B)
        packed = two[3, rows, :] + in2[0, rows, :] + in2[1, rows, :] + in2[2, rows, :]
        row = pl.ds(2 * B + 2 * second + h, 1)
        diag = two[3, row, :] + in2[0, row, :] + in2[1, row, :] + in2[2, row, :]
        m0 = jnp.where(upper, jnp.where(on_diag, packed, 2.0 * packed), 0.0)
        m1 = jnp.where(upper, jnp.where(on_diag, jnp.broadcast_to(diag, (B, B)), 0.0), 2.0 * packed)
        for l, m in ((0, m0), (1, m1)):
            q = qbuf[h, l]
            zs[2 * h + l : 2 * h + l + 1, :] = jnp.sum(q * dot(m, q, 1, 0, HIGHEST), axis=0, keepdims=True)
    z_copies = []
    for k in range(1, 8):
        copy = remote(zs, zr.at[k], s_z.at[k - 1], r_z.at[k - 1], at((z + k) % 8, y, x, c))
        copy.start()
        z_copies.append(copy)
    zr[0] = zs[...]

    @pl.when(side == 1)
    def _():
        qa_copy.wait_recv()

    loads[4].wait()
    for l in range(2):
        rot[l] = dot(qa[l], gs[l].astype(F32), 0, 0, HIGHEST)

    for copy in z_copies:
        copy.wait_recv()
    scales = zr[0]
    for k in range(1, 8):
        scales = scales + zr[k]
    scales = scales / total_rows
    keep[...] = scales

    xy_copies = []
    for k in range(1, 16):
        n = (row_col + k) % 16
        xy_copies.append(remote(zs, sg.at[x], s_xy.at[k - 1], r_xy.at[x], at(z, n // 4, n % 4, c)))
    sa_copy = remote(zs, sa, s_p.at[1], r_p.at[1], partner)

    for copy in z_copies:
        copy.wait_send()

    @pl.when(is_source)
    def _():
        zs[:2, :] = keep[pl.ds(2 * half_here, 2), :]
        for copy in xy_copies:
            copy.start()
        sg[x] = zs[...]

    @pl.when(side == 0)
    def _():
        zs[:2, :] = keep[pl.ds(2 * z_hi, 2), :]
        sa_copy.start()
        sa[...] = zs[...]

    @pl.when(side == 1)
    def _():
        sa_copy.wait_recv()

    for k in range(1, 4):
        from_x = (x + 4 - k) % 4
        remote(qg.at[x], qg.at[from_x], s_qx.at[k - 1], r_qx.at[k - 1], partner).wait_recv()
    for l in range(2):
        for q in range(4):
            cols = slice(q * B, (q + 1) * B)
            inner_s[l, :, cols] = dot(rot[l, :, cols], qg[q, l], 1, 0, HIGHEST)

    for q in range(4):
        @pl.when(jnp.logical_not(jnp.logical_and(is_source, x == q)))
        def _():
            remote(zs, sg.at[q], s_xy.at[0], r_xy.at[q], partner).wait_recv()

    for l in range(2):
        left = jnp.transpose(jnp.broadcast_to(sa[l : l + 1, :], (B, B)))
        for q in range(4):
            cols = slice(q * B, (q + 1) * B)
            scaled = inner_s[l, :, cols] / (left * sg[q, l : l + 1, :] + DAMPING)
            inner_s[l, :, cols] = dot(scaled, qg[q, l], 1, 1, HIGHEST)
        out[l] = dot(qa[l], inner_s[l], 1, 0, HIGHEST).astype(out.dtype)

    for copy in [core_q] + core_copies + one_copies + rs_copies + ag_copies + two_copies + qx_copies:
        copy.wait_send()

    @pl.when(is_source)
    def _():
        for copy in qy_copies + xy_copies:
            copy.wait_send()

    @pl.when(side == 0)
    def _():
        qa_copy.wait_send()
        sa_copy.wait_send()


def body(acts, grads_out, grad, bases_a, bases_g, owner_slot):
    rows = acts.shape[1]
    total_rows = rows * lax.axis_size("dp") * lax.axis_size("factor")
    dma = pltpu.SemaphoreType.DMA
    scratch = [
        pltpu.VMEM((2,) + acts.shape, acts.dtype),
        pltpu.VMEM(grad.shape, grad.dtype),
        pltpu.VMEM((2,) + bases_a.shape, F32),
        pltpu.VMEM((4, CHUNK, B), F32),
        pltpu.VMEM((4, CHUNK, B), F32),
        pltpu.VMEM((4, CHUNK, B), F32),
        pltpu.VMEM((3, 8 * B, B), jnp.int16),
        pltpu.VMEM((3, SIDE, B), F32),
        pltpu.VMEM((3, 8 * B, B), jnp.int16),
        pltpu.VMEM((3, SIDE, B), F32),
        pltpu.VMEM((4, PIECE, B), F32),
        pltpu.VMEM((3, PIECE, B), F32),
        pltpu.VMEM((2, 2, B, B), F32),
        pltpu.VMEM((2, B, B), F32),
        pltpu.VMEM((2, B, B), F32),
        pltpu.VMEM((3, 2, 32, B), F32),
        pltpu.VMEM((2, 32, B), F32),
        pltpu.VMEM((2, 2, B, B), F32),
        pltpu.VMEM((2, B, B), F32),
        pltpu.VMEM((4, 2, B, B), F32),
        pltpu.VMEM((8, B), F32),
        pltpu.VMEM((8, 8, B), F32),
        pltpu.VMEM((8, B), F32),
        pltpu.VMEM((4, 8, B), F32),
        pltpu.VMEM((8, B), F32),
        pltpu.VMEM((2, B, 4 * B), F32),
        pltpu.VMEM((2, B, 4 * B), F32),
        dma((5,)),
        dma((4,)), dma((4,)),
        dma((3,)), dma((3,)),
        dma((3,)), dma((3,)),
        dma((3,)), dma((3,)),
        dma, dma,
        dma((3,)), dma((3,)),
        dma((7,)), dma((7,)),
        dma((3,)), dma,
        dma((3,)), dma((3,)),
        dma((7,)), dma((7,)),
        dma((15,)), dma((4,)),
        dma((2,)), dma((2,)),
    ]
    hbm = pl.BlockSpec(memory_space=pltpu.HBM)
    return pl.pallas_call(
        functools.partial(kernel, total_rows),
        out_shape=jax.ShapeDtypeStruct(grad.shape, jnp.bfloat16),
        in_specs=[pl.BlockSpec(memory_space=pltpu.SMEM)] + [hbm] * 5,
        out_specs=pl.BlockSpec(memory_space=pltpu.VMEM),
        scratch_shapes=scratch,
        compiler_params=pltpu.CompilerParams(
            collective_id=0, has_side_effects=True, vmem_limit_bytes=63 * 1024 * 1024
        ),
        cost_estimate=pl.CostEstimate(flops=2 * 10**9, bytes_accessed=10**7, transcendentals=0),
    )(owner_slot, acts, grads_out, grad, bases_a, bases_g)


def solution(mesh):
    tokens = P(None, ("factor", "dp"), None)
    bases = P("factor", "dp", None)
    split = P(None, "dp", "factor")
    in_specs = (tokens, tokens, split, bases, bases, P())
    return jax.shard_map(body, mesh=mesh, in_specs=in_specs, out_specs=split, check_vma=False)
```

```python
import functools

import jax
import jax.numpy as jnp
from jax import lax
from jax.experimental import pallas as pl
from jax.experimental.pallas import tpu as pltpu
from jax.sharding import PartitionSpec as P

MESH = pl.DeviceIdType.MESH
B = 128
SLOTS = 2
DAMPING = 0.05
HIGHEST = lax.Precision.HIGHEST
F32 = jnp.float32

GROUP = 8 * B + 8
SET = 4 * B
ORDER = (2, 1, 3, 0)
SIDE = 16
FULL = 32500.0
TINY = 1e-37


def dot(a, b, ca, cb, precision=None):
    return lax.dot_general(a, b, (((ca,), (cb,)), ((), ())), precision=precision, preferred_element_type=F32)


def kernel(total_rows, slot_ref, acts, grads, grad, bases_a, bases_g, out,
           xs, gs, bs, part, core_in, own, code, norm, in_code, in_norm, in_two, in_row, row_sum, qc, qc_in, qs, qs_in, qm, qbuf, qa, qg,
           zs, zr, sa, sg, keep, rot, inner_s,
           ld, s_core, r_core, s_one, r_one, s_norm, r_norm, s_two, r_two, s_row, r_row, s_q, r_q, s_rs, r_rs, s_ag, r_ag,
           s_qy, r_qy, s_qx, r_qx, s_z, r_z, s_xy, r_xy, s_p, r_p):
    f = lax.axis_index("factor")
    d = lax.axis_index("dp")
    z_lo, c = f // 2, f % 2
    z_hi, y, x = d // 16, (d // 4) % 4, d % 4
    z = 4 * z_hi + z_lo
    other = 1 - c
    side = 1 - (y + c) % 2
    source_row = 2 * (z_lo % 2) + c
    is_source = y == source_row
    half_here = z_lo // 2

    def at(zz, yy, xx, cc):
        return (2 * (zz % 4) + cc, 16 * (zz // 4) + 4 * yy + xx)

    def column(k):
        return (y + (k + 1) // 4) % 4, (x + (k + 1) % 4) % 4

    def block(g, m):
        if m < 4:
            return 0, m, (x + ORDER[g]) % 4
        return 1, (y + ORDER[g]) % 4, m - 4

    def along(first, k):
        return at(z, y, (x + ORDER[k]) % 4, c) if first == 0 else at(z, (y + ORDER[k]) % 4, x, c)

    def remote(src, dst, send, recv, to):
        return pltpu.make_async_remote_copy(src_ref=src, dst_ref=dst, send_sem=send, recv_sem=recv,
                                            device_id=to, device_id_type=MESH)

    partner = at(z, y, x, other)
    barrier = pltpu.get_barrier_semaphore()

    def signal(to):
        pl.semaphore_signal(barrier, inc=1, device_id=to, device_id_type=MESH)

    signal(partner)
    for k in range(15):
        signal(at(z, *column(k), c))
    for k in range(1, 8):
        signal(at((z + k) % 8, y, x, c))

    load_a = pltpu.make_async_copy(bases_a, bs.at[0], ld.at[4])
    load_g = pltpu.make_async_copy(bases_g, bs.at[1], ld.at[5])
    load_grad = pltpu.make_async_copy(grad, gs, ld.at[6])

    def load_group(g):
        for m in range(8):
            h, yb, xb = block(g, m)
            cols = pl.ds(pl.multiple_of((16 * h + 4 * yb + xb) * B, B), B)
            for sd, tokens in ((0, acts), (1, grads)):
                pltpu.make_async_copy(tokens.at[:, :, cols], xs.at[g, m, sd], ld.at[g]).start()

    load_a.start()
    load_g.start()
    load_group(0)
    load_group(1)

    load_a.wait()
    load_g.wait()
    for l in range(2):
        slot = slot_ref[l]
        mine = (slot // SLOTS) == f
        for which, sd in ((0, side), (1, 1 - side)):
            picked = jnp.where(slot % SLOTS == 0, bs[sd, 0], bs[sd, 1])
            qc[which, l] = jnp.where(mine, picked, jnp.zeros_like(picked))
    norm[...] = jnp.zeros_like(norm)
    row_sum[...] = jnp.zeros_like(row_sum)
    pl.semaphore_wait(barrier, 23)

    core_q = remote(qc.at[1], qc_in, s_q, r_q, partner)
    core_q.start()
    load_group(2)
    load_group(3)
    load_grad.start()

    iota_r = lax.broadcasted_iota(jnp.int32, (B, B), 0)
    iota_c = lax.broadcasted_iota(jnp.int32, (B, B), 1)
    iota_16 = lax.broadcasted_iota(jnp.int32, (16, B), 0)
    upper = iota_r <= iota_c
    on_diag = iota_r == iota_c

    def norms_of(tile, row0, row1):
        right = tile.astype(jnp.bfloat16)

        def outer(row):
            return dot(jnp.where(iota_16 == row, tile, 0.0).astype(jnp.bfloat16), right, 0, 0)

        return jnp.where(upper, outer(row0), outer(row1))

    def terms(core, g, dst, add):
        for m in range(8):
            yb = block(g, m)[1]
            sd = 1 - (yb + core) % 2
            x0 = xs[g, m, sd, 0]
            x1 = xs[g, m, sd, 1]
            f0 = dot(x0, x0, 0, 0)
            f1 = dot(x1, x1, 0, 0)
            packed = jnp.where(upper, f0, f1)
            diag = jnp.sum(jnp.where(on_diag, f1, 0.0), axis=0, keepdims=True)
            rows = slice(m * B, (m + 1) * B)
            row = slice(8 * B + m, 8 * B + m + 1)
            if add is not None:
                packed = packed + add[rows, :]
                diag = diag + add[row, :]
            dst[rows, :] = packed
            dst[row, :] = diag

    core_copies, one_copies = [], []

    def for_partner(g):
        pltpu.make_async_copy(xs.at[g], xs.at[g], ld.at[g]).wait()
        terms(other, g, part.at[g], None)
        copy = remote(part.at[g], core_in.at[g], s_core.at[g], r_core.at[g], partner)
        copy.start()
        core_copies.append(copy)

    def for_plane(g):
        core_copies[g].wait_recv()
        terms(c, g, own.at[g], core_in.at[g])
        if g == 3:
            for w in range(2):
                row_sum[w, 0:4, :] = own[g, 8 * B + 4 * w : 8 * B + 4 * w + 4, :]
            return
        diag0 = [jnp.sum(jnp.where(on_diag, own[g, m * B : (m + 1) * B, :], 0.0), axis=0, keepdims=True)
                 for m in range(8)]
        diag1 = own[g, 8 * B :, :]
        diag = jnp.concatenate(diag0 + [diag1], axis=0)
        inverse = jnp.where(diag > TINY, lax.rsqrt(jnp.maximum(diag, TINY)), 1.0)
        tile = inverse.astype(jnp.bfloat16).astype(F32)
        for w in range(2):
            norm[w, g, 0:4, :] = tile[4 * w : 4 * w + 4, :]
            norm[w, g, 4:8, :] = tile[8 + 4 * w : 12 + 4 * w, :]
            norm[w, g, 8:12, :] = diag1[4 * w : 4 * w + 4, :]
            for i in range(4):
                m = 4 * w + i
                unit = own[g, m * B : (m + 1) * B, :] * norms_of(tile, m, 8 + m)
                code[w, g, i * B : (i + 1) * B, :] = jnp.round(unit * FULL).astype(jnp.int32).astype(jnp.int16)
            to = along(w, g)
            pair = (remote(norm.at[w, g], in_norm.at[w, g], s_norm.at[w, g], r_norm.at[w, g], to),
                    remote(code.at[w, g], in_code.at[w, g], s_one.at[w, g], r_one.at[w, g], to))
            for copy in pair:
                copy.start()
            one_copies.append(pair)

    def decode(w, g):
        for copy in one_copies[2 * g + w]:
            copy.wait_recv()
        tile = in_norm[w, g]
        for i in range(4):
            unit = in_code[w, g, i * B : (i + 1) * B, :].astype(jnp.int32).astype(F32) * (1.0 / FULL)
            own[3, (4 * w + i) * B : (4 * w + i + 1) * B, :] += unit / norms_of(tile, i, 4 + i)
        row_sum[w, 0:4, :] += in_norm[w, g, 8:12, :]

    two_copies = []

    def second(w):
        for k in range(3):
            to = along(1 - w, k)
            u = ((y, x)[w] + ORDER[k]) % 4
            rows = pl.ds(pl.multiple_of((4 * w + u) * B, B), B)
            for copy in (remote(row_sum.at[w], in_row.at[w, k], s_row.at[w, k], r_row.at[w, k], to),
                         remote(own.at[3, rows, :], in_two.at[w, k], s_two.at[w, k], r_two.at[w, k], to)):
                copy.start()
                two_copies.append(copy)

    for_partner(0)

    core_q.wait_recv()
    for l in range(2):
        qs[l] = qc[0, l] + qc_in[l]
    rs_copies = []
    for k in range(1, 4):
        zz = (z_lo + k) % 4
        copy = remote(qs.at[:, pl.ds(pl.multiple_of(32 * zz, 32), 32), :], qs_in.at[k - 1],
                      s_rs.at[k - 1], r_rs.at[k - 1], at(4 * z_hi + zz, y, x, c))
        copy.start()
        rs_copies.append(copy)

    for_partner(1)
    for_plane(0)
    for_partner(2)
    for_plane(1)
    for_partner(3)

    for copy in rs_copies:
        copy.wait_recv()
    here = pl.ds(pl.multiple_of(32 * z_lo, 32), 32)
    summed = qs[:, here, :] + qs_in[0] + qs_in[1] + qs_in[2]
    qm[...] = summed
    qbuf[z_hi, :, here, :] = summed
    ag_copies = []
    for k in range(1, 8):
        copy = remote(qm, qbuf.at[z_hi, :, here, :], s_ag.at[k - 1], r_ag.at[k - 1], at((z + k) % 8, y, x, c))
        copy.start()
        ag_copies.append(copy)

    for_plane(2)
    for_plane(3)
    for g in range(3):
        for w in range(2):
            decode(w, g)
            if g == 2:
                second(w)

    for k in range(1, 8):
        zz = (z + 8 - k) % 8
        rows = pl.ds(pl.multiple_of(32 * (zz % 4), 32), 32)
        remote(qm, qbuf.at[zz // 4, :, rows, :], s_ag.at[k - 1], r_ag.at[k - 1], partner).wait_recv()

    qy_copies = []
    for k in range(1, 4):
        copy = remote(qbuf.at[half_here], qg.at[x], s_qy.at[k - 1], r_qy, at(z, (y + k) % 4, x, c))
        qy_copies.append(copy)
    qa_copy = remote(qbuf.at[z_hi], qa, s_p.at[0], r_p.at[0], partner)

    @pl.when(is_source)
    def _():
        for copy in qy_copies:
            copy.start()
        qg[x] = qbuf[half_here]

    @pl.when(side == 0)
    def _():
        qa_copy.start()
        qa[...] = qbuf[z_hi]

    for copy in two_copies:
        copy.wait_recv()
    zs[...] = jnp.zeros_like(zs)
    for h in range(2):
        u = 4 * h + (y, x)[h]
        packed = own[3, pl.ds(pl.multiple_of(u * B, B), B), :] + in_two[h, 0] + in_two[h, 1] + in_two[h, 2]
        row = pl.ds((y, x)[h], 1)
        diag = row_sum[h, row, :] + in_row[h, 0, row, :] + in_row[h, 1, row, :] + in_row[h, 2, row, :]
        m0 = jnp.where(upper, jnp.where(on_diag, packed, 2.0 * packed), 0.0)
        m1 = jnp.where(upper, jnp.where(on_diag, jnp.broadcast_to(diag, (B, B)), 0.0), 2.0 * packed)
        for l, m in ((0, m0), (1, m1)):
            q = qbuf[h, l]
            zs[2 * h + l : 2 * h + l + 1, :] = jnp.sum(q * dot(m, q, 1, 0, HIGHEST), axis=0, keepdims=True)
    z_copies = []
    for k in range(1, 8):
        copy = remote(zs, zr.at[k], s_z.at[k - 1], r_z.at[k - 1], at((z + k) % 8, y, x, c))
        copy.start()
        z_copies.append(copy)
    zr[0] = zs[...]

    @pl.when(jnp.logical_not(is_source))
    def _():
        qy_copies[0].wait_recv()

    qx_copies = []
    for k in range(1, 4):
        copy = remote(qg.at[x], qg.at[x], s_qx.at[k - 1], r_qx.at[k - 1], at(z, y, (x + k) % 4, c))
        copy.start()
        qx_copies.append(copy)

    @pl.when(side == 1)
    def _():
        qa_copy.wait_recv()

    load_grad.wait()
    for l in range(2):
        rot[l] = dot(qa[l], gs[l].astype(F32), 0, 0, HIGHEST)

    for copy in z_copies:
        copy.wait_recv()
    scales = zr[0]
    for k in range(1, 8):
        scales = scales + zr[k]
    scales = scales / total_rows
    keep[...] = scales

    xy_copies = []
    for k in range(15):
        xy_copies.append(remote(zs, sg.at[x], s_xy.at[k], r_xy.at[x], at(z, *column(k), c)))
    sa_copy = remote(zs, sa, s_p.at[1], r_p.at[1], partner)

    for copy in z_copies:
        copy.wait_send()

    @pl.when(is_source)
    def _():
        zs[:2, :] = keep[pl.ds(2 * half_here, 2), :]
        for copy in xy_copies:
            copy.start()
        sg[x] = zs[...]

    @pl.when(side == 0)
    def _():
        zs[:2, :] = keep[pl.ds(2 * z_hi, 2), :]
        sa_copy.start()
        sa[...] = zs[...]

    @pl.when(side == 1)
    def _():
        sa_copy.wait_recv()

    def turn(q):
        cols = pl.ds(pl.multiple_of(q * B, B), B)
        for l in range(2):
            inner_s[l, :, cols] = dot(rot[l, :, cols], qg[q, l], 1, 0, HIGHEST)

    turn(x)
    for k in (1, 3, 2):
        from_x = (x + 4 - k) % 4
        remote(qg.at[x], qg.at[from_x], s_qx.at[k - 1], r_qx.at[k - 1], partner).wait_recv()
        turn(from_x)

    for q in range(4):
        @pl.when(jnp.logical_not(jnp.logical_and(is_source, x == q)))
        def _():
            remote(zs, sg.at[q], s_xy.at[0], r_xy.at[q], partner).wait_recv()

    for l in range(2):
        left = jnp.transpose(jnp.broadcast_to(sa[l : l + 1, :], (B, B)))
        for q in range(4):
            cols = slice(q * B, (q + 1) * B)
            scaled = inner_s[l, :, cols] / (left * sg[q, l : l + 1, :] + DAMPING)
            inner_s[l, :, cols] = dot(scaled, qg[q, l], 1, 1, HIGHEST)
        out[l] = dot(qa[l], inner_s[l], 1, 0, HIGHEST).astype(out.dtype)

    for pair in one_copies:
        for copy in pair:
            copy.wait_send()
    for copy in [core_q] + core_copies + two_copies + rs_copies + ag_copies + qx_copies:
        copy.wait_send()

    @pl.when(is_source)
    def _():
        for copy in qy_copies + xy_copies:
            copy.wait_send()

    @pl.when(side == 0)
    def _():
        qa_copy.wait_send()
        sa_copy.wait_send()


def body(acts, grads_out, grad, bases_a, bases_g, owner_slot):
    rows = acts.shape[1]
    total_rows = rows * lax.axis_size("dp") * lax.axis_size("factor")
    dma = pltpu.SemaphoreType.DMA
    scratch = [
        pltpu.VMEM((4, 8, 2, 2, rows, B), acts.dtype),
        pltpu.VMEM(grad.shape, grad.dtype),
        pltpu.VMEM((2,) + bases_a.shape, F32),
        pltpu.VMEM((4, GROUP, B), F32),
        pltpu.VMEM((4, GROUP, B), F32),
        pltpu.VMEM((4, GROUP, B), F32),
        pltpu.VMEM((2, 3, SET, B), jnp.int16),
        pltpu.VMEM((2, 3, SIDE, B), F32),
        pltpu.VMEM((2, 3, SET, B), jnp.int16),
        pltpu.VMEM((2, 3, SIDE, B), F32),
        pltpu.VMEM((2, 3, B, B), F32),
        pltpu.VMEM((2, 3, 8, B), F32),
        pltpu.VMEM((2, 8, B), F32),
        pltpu.VMEM((2, 2, B, B), F32),
        pltpu.VMEM((2, B, B), F32),
        pltpu.VMEM((2, B, B), F32),
        pltpu.VMEM((3, 2, 32, B), F32),
        pltpu.VMEM((2, 32, B), F32),
        pltpu.VMEM((2, 2, B, B), F32),
        pltpu.VMEM((2, B, B), F32),
        pltpu.VMEM((4, 2, B, B), F32),
        pltpu.VMEM((8, B), F32),
        pltpu.VMEM((8, 8, B), F32),
        pltpu.VMEM((8, B), F32),
        pltpu.VMEM((4, 8, B), F32),
        pltpu.VMEM((8, B), F32),
        pltpu.VMEM((2, B, 4 * B), F32),
        pltpu.VMEM((2, B, 4 * B), F32),
        dma((7,)),
        dma((4,)), dma((4,)),
        dma((2, 3)), dma((2, 3)),
        dma((2, 3)), dma((2, 3)),
        dma((2, 3)), dma((2, 3)),
        dma((2, 3)), dma((2, 3)),
        dma, dma,
        dma((3,)), dma((3,)),
        dma((7,)), dma((7,)),
        dma((3,)), dma,
        dma((3,)), dma((3,)),
        dma((7,)), dma((7,)),
        dma((15,)), dma((4,)),
        dma((2,)), dma((2,)),
    ]
    hbm = pl.BlockSpec(memory_space=pltpu.HBM)
    return pl.pallas_call(
        functools.partial(kernel, total_rows),
        out_shape=jax.ShapeDtypeStruct(grad.shape, jnp.bfloat16),
        in_specs=[pl.BlockSpec(memory_space=pltpu.SMEM)] + [hbm] * 5,
        out_specs=pl.BlockSpec(memory_space=pltpu.VMEM),
        scratch_shapes=scratch,
        compiler_params=pltpu.CompilerParams(
            collective_id=0, has_side_effects=True, vmem_limit_bytes=63 * 1024 * 1024
        ),
        cost_estimate=pl.CostEstimate(flops=2 * 10**9, bytes_accessed=10**7, transcendentals=0),
    )(owner_slot, acts, grads_out, grad, bases_a, bases_g)


def solution(mesh):
    tokens = P(None, ("factor", "dp"), None)
    bases = P("factor", "dp", None)
    split = P(None, "dp", "factor")
    in_specs = (tokens, tokens, split, bases, bases, P())
    return jax.shard_map(body, mesh=mesh, in_specs=in_specs, out_specs=split, check_vma=False)
```

```python
import functools

import jax
import jax.numpy as jnp
from jax import lax
from jax.experimental import pallas as pl
from jax.experimental.pallas import tpu as pltpu
from jax.sharding import PartitionSpec as P

MESH = pl.DeviceIdType.MESH
B = 128
SLOTS = 2
DAMPING = 0.05
F32 = jnp.float32

GROUP = 8 * B + 8
SET = 4 * B
ORDER = (2, 1, 3, 0)
SIDE = 16
FULL = 32500.0
TINY = 1e-37


def dot(a, b, ca, cb, precision=None):
    return lax.dot_general(a, b, (((ca,), (cb,)), ((), ())), precision=precision, preferred_element_type=F32)


def halves(a):
    high = a.astype(jnp.bfloat16)
    return high, (a - high.astype(F32)).astype(jnp.bfloat16)


def dot3(a, b, ca, cb):
    (ah, al), (bh, bl) = halves(a), halves(b)
    return dot(ah, bh, ca, cb) + (dot(ah, bl, ca, cb) + dot(al, bh, ca, cb))


def kernel(total_rows, slot_ref, acts, grads, grad, bases_a, bases_g, out,
           xs, gs, bs, part, core_in, own, code, norm, in_code, in_norm, in_two, in_row, row_sum, qc, qc_in, qs, qs_in, qm, qbuf, qa, qg,
           zs, zr, sa, sg, keep, rot, inner_s,
           ld, s_core, r_core, s_one, r_one, s_norm, r_norm, s_two, r_two, s_row, r_row, s_q, r_q, s_rs, r_rs, s_ag, r_ag,
           s_qy, r_qy, s_qx, r_qx, s_z, r_z, s_xy, r_xy, s_p, r_p):
    f = lax.axis_index("factor")
    d = lax.axis_index("dp")
    z_lo, c = f // 2, f % 2
    z_hi, y, x = d // 16, (d // 4) % 4, d % 4
    z = 4 * z_hi + z_lo
    other = 1 - c
    side = 1 - (y + c) % 2
    source_row = 2 * (z_lo % 2) + c
    is_source = y == source_row
    half_here = z_lo // 2

    def at(zz, yy, xx, cc):
        return (2 * (zz % 4) + cc, 16 * (zz // 4) + 4 * yy + xx)

    def column(k):
        return (y + (k + 1) // 4) % 4, (x + (k + 1) % 4) % 4

    def block(g, m):
        if m < 4:
            return 0, m, (x + ORDER[g]) % 4
        return 1, (y + ORDER[g]) % 4, m - 4

    def along(first, k):
        return at(z, y, (x + ORDER[k]) % 4, c) if first == 0 else at(z, (y + ORDER[k]) % 4, x, c)

    def remote(src, dst, send, recv, to):
        return pltpu.make_async_remote_copy(src_ref=src, dst_ref=dst, send_sem=send, recv_sem=recv,
                                            device_id=to, device_id_type=MESH)

    partner = at(z, y, x, other)
    barrier = pltpu.get_barrier_semaphore()

    def signal(to):
        pl.semaphore_signal(barrier, inc=1, device_id=to, device_id_type=MESH)

    signal(partner)
    for k in range(15):
        signal(at(z, *column(k), c))
    for k in range(1, 8):
        signal(at((z + k) % 8, y, x, c))

    load_a = pltpu.make_async_copy(bases_a, bs.at[0], ld.at[4])
    load_g = pltpu.make_async_copy(bases_g, bs.at[1], ld.at[5])
    load_grad = pltpu.make_async_copy(grad, gs, ld.at[6])

    def load_group(g):
        for m in range(8):
            h, yb, xb = block(g, m)
            cols = pl.ds(pl.multiple_of((16 * h + 4 * yb + xb) * B, B), B)
            for sd, tokens in ((0, acts), (1, grads)):
                pltpu.make_async_copy(tokens.at[:, :, cols], xs.at[g, m, sd], ld.at[g]).start()

    load_a.start()
    load_g.start()
    load_group(0)
    load_group(1)

    load_a.wait()
    load_g.wait()
    for l in range(2):
        slot = slot_ref[l]
        mine = (slot // SLOTS) == f
        for which, sd in ((0, side), (1, 1 - side)):
            picked = jnp.where(slot % SLOTS == 0, bs[sd, 0], bs[sd, 1])
            qc[which, l] = jnp.where(mine, picked, jnp.zeros_like(picked))
    norm[...] = jnp.zeros_like(norm)
    row_sum[...] = jnp.zeros_like(row_sum)
    pl.semaphore_wait(barrier, 23)

    core_q = remote(qc.at[1], qc_in, s_q, r_q, partner)
    core_q.start()
    load_group(2)
    load_group(3)
    load_grad.start()

    iota_r = lax.broadcasted_iota(jnp.int32, (B, B), 0)
    iota_c = lax.broadcasted_iota(jnp.int32, (B, B), 1)
    iota_16 = lax.broadcasted_iota(jnp.int32, (16, B), 0)
    upper = iota_r <= iota_c
    on_diag = iota_r == iota_c

    def norms_of(tile, row0, row1):
        right = tile.astype(jnp.bfloat16)

        def outer(row):
            return dot(jnp.where(iota_16 == row, tile, 0.0).astype(jnp.bfloat16), right, 0, 0)

        return jnp.where(upper, outer(row0), outer(row1))

    def terms(core, g, dst, add):
        for m in range(8):
            yb = block(g, m)[1]
            sd = 1 - (yb + core) % 2
            x0 = xs[g, m, sd, 0]
            x1 = xs[g, m, sd, 1]
            f0 = dot(x0, x0, 0, 0)
            f1 = dot(x1, x1, 0, 0)
            packed = jnp.where(upper, f0, f1)
            diag = jnp.sum(jnp.where(on_diag, f1, 0.0), axis=0, keepdims=True)
            rows = slice(m * B, (m + 1) * B)
            row = slice(8 * B + m, 8 * B + m + 1)
            if add is not None:
                packed = packed + add[rows, :]
                diag = diag + add[row, :]
            dst[rows, :] = packed
            dst[row, :] = diag

    core_copies, one_copies = [], []

    def for_partner(g):
        pltpu.make_async_copy(xs.at[g], xs.at[g], ld.at[g]).wait()
        terms(other, g, part.at[g], None)
        copy = remote(part.at[g], core_in.at[g], s_core.at[g], r_core.at[g], partner)
        copy.start()
        core_copies.append(copy)

    def for_plane(g):
        core_copies[g].wait_recv()
        terms(c, g, own.at[g], core_in.at[g])
        if g == 3:
            for w in range(2):
                row_sum[w, 0:4, :] = own[g, 8 * B + 4 * w : 8 * B + 4 * w + 4, :]
            return
        diag0 = [jnp.sum(jnp.where(on_diag, own[g, m * B : (m + 1) * B, :], 0.0), axis=0, keepdims=True)
                 for m in range(8)]
        diag1 = own[g, 8 * B :, :]
        diag = jnp.concatenate(diag0 + [diag1], axis=0)
        inverse = jnp.where(diag > TINY, lax.rsqrt(jnp.maximum(diag, TINY)), 1.0)
        tile = inverse.astype(jnp.bfloat16).astype(F32)
        for w in range(2):
            norm[w, g, 0:4, :] = tile[4 * w : 4 * w + 4, :]
            norm[w, g, 4:8, :] = tile[8 + 4 * w : 12 + 4 * w, :]
            norm[w, g, 8:12, :] = diag1[4 * w : 4 * w + 4, :]
            for i in range(4):
                m = 4 * w + i
                unit = own[g, m * B : (m + 1) * B, :] * norms_of(tile, m, 8 + m)
                code[w, g, i * B : (i + 1) * B, :] = jnp.round(unit * FULL).astype(jnp.int32).astype(jnp.int16)
            to = along(w, g)
            pair = (remote(norm.at[w, g], in_norm.at[w, g], s_norm.at[w, g], r_norm.at[w, g], to),
                    remote(code.at[w, g], in_code.at[w, g], s_one.at[w, g], r_one.at[w, g], to))
            for copy in pair:
                copy.start()
            one_copies.append(pair)

    def decode(w, g):
        for copy in one_copies[2 * g + w]:
            copy.wait_recv()
        tile = in_norm[w, g]
        for i in range(4):
            unit = in_code[w, g, i * B : (i + 1) * B, :].astype(jnp.int32).astype(F32) * (1.0 / FULL)
            own[3, (4 * w + i) * B : (4 * w + i + 1) * B, :] += unit / norms_of(tile, i, 4 + i)
        row_sum[w, 0:4, :] += in_norm[w, g, 8:12, :]

    two_copies = []

    def second(w):
        for k in range(3):
            to = along(1 - w, k)
            u = ((y, x)[w] + ORDER[k]) % 4
            rows = pl.ds(pl.multiple_of((4 * w + u) * B, B), B)
            for copy in (remote(row_sum.at[w], in_row.at[w, k], s_row.at[w, k], r_row.at[w, k], to),
                         remote(own.at[3, rows, :], in_two.at[w, k], s_two.at[w, k], r_two.at[w, k], to)):
                copy.start()
                two_copies.append(copy)

    for_partner(0)

    core_q.wait_recv()
    for l in range(2):
        qs[l] = qc[0, l] + qc_in[l]
    rs_copies = []
    for k in range(1, 4):
        zz = (z_lo + k) % 4
        copy = remote(qs.at[:, pl.ds(pl.multiple_of(32 * zz, 32), 32), :], qs_in.at[k - 1],
                      s_rs.at[k - 1], r_rs.at[k - 1], at(4 * z_hi + zz, y, x, c))
        copy.start()
        rs_copies.append(copy)

    for_partner(1)
    for_plane(0)
    for_partner(2)
    for_plane(1)
    for_partner(3)

    for_plane(2)

    for copy in rs_copies:
        copy.wait_recv()
    here = pl.ds(pl.multiple_of(32 * z_lo, 32), 32)
    summed = qs[:, here, :] + qs_in[0] + qs_in[1] + qs_in[2]
    qm[...] = summed
    qbuf[z_hi, :, here, :] = summed
    ag_copies = []
    for k in range(1, 8):
        copy = remote(qm, qbuf.at[z_hi, :, here, :], s_ag.at[k - 1], r_ag.at[k - 1], at((z + k) % 8, y, x, c))
        copy.start()
        ag_copies.append(copy)

    for_plane(3)
    for g in range(3):
        for w in range(2):
            decode(w, g)
            if g == 2:
                second(w)

    for k in range(1, 8):
        zz = (z + 8 - k) % 8
        rows = pl.ds(pl.multiple_of(32 * (zz % 4), 32), 32)
        remote(qm, qbuf.at[zz // 4, :, rows, :], s_ag.at[k - 1], r_ag.at[k - 1], partner).wait_recv()

    qy_copies = []
    for k in range(1, 4):
        copy = remote(qbuf.at[half_here], qg.at[x], s_qy.at[k - 1], r_qy, at(z, (y + k) % 4, x, c))
        qy_copies.append(copy)
    qa_copy = remote(qbuf.at[z_hi], qa, s_p.at[0], r_p.at[0], partner)

    @pl.when(is_source)
    def _():
        for copy in qy_copies:
            copy.start()
        qg[x] = qbuf[half_here]

    @pl.when(side == 0)
    def _():
        qa_copy.start()
        qa[...] = qbuf[z_hi]

    for copy in two_copies:
        copy.wait_recv()
    zs[...] = jnp.zeros_like(zs)
    for h in range(2):
        u = 4 * h + (y, x)[h]
        packed = own[3, pl.ds(pl.multiple_of(u * B, B), B), :] + in_two[h, 0] + in_two[h, 1] + in_two[h, 2]
        row = pl.ds((y, x)[h], 1)
        diag = row_sum[h, row, :] + in_row[h, 0, row, :] + in_row[h, 1, row, :] + in_row[h, 2, row, :]
        m0 = jnp.where(upper, jnp.where(on_diag, packed, 2.0 * packed), 0.0)
        m1 = jnp.where(upper, jnp.where(on_diag, jnp.broadcast_to(diag, (B, B)), 0.0), 2.0 * packed)
        for l, m in ((0, m0), (1, m1)):
            q = qbuf[h, l]
            zs[2 * h + l : 2 * h + l + 1, :] = jnp.sum(q * dot3(m, q, 1, 0), axis=0, keepdims=True)
    z_copies = []
    for k in range(1, 8):
        copy = remote(zs, zr.at[k], s_z.at[k - 1], r_z.at[k - 1], at((z + k) % 8, y, x, c))
        copy.start()
        z_copies.append(copy)
    zr[0] = zs[...]

    @pl.when(jnp.logical_not(is_source))
    def _():
        qy_copies[0].wait_recv()

    qx_copies = []
    for k in range(1, 4):
        copy = remote(qg.at[x], qg.at[x], s_qx.at[k - 1], r_qx.at[k - 1], at(z, y, (x + k) % 4, c))
        copy.start()
        qx_copies.append(copy)

    @pl.when(side == 1)
    def _():
        qa_copy.wait_recv()

    load_grad.wait()
    for l in range(2):
        high, low = halves(qa[l])
        rot[l] = dot(high, gs[l], 0, 0) + dot(low, gs[l], 0, 0)

    for copy in z_copies:
        copy.wait_recv()
    scales = zr[0]
    for k in range(1, 8):
        scales = scales + zr[k]
    scales = scales / total_rows
    keep[...] = scales

    xy_copies = []
    for k in range(15):
        xy_copies.append(remote(zs, sg.at[x], s_xy.at[k], r_xy.at[x], at(z, *column(k), c)))
    sa_copy = remote(zs, sa, s_p.at[1], r_p.at[1], partner)

    for copy in z_copies:
        copy.wait_send()

    @pl.when(is_source)
    def _():
        zs[:2, :] = keep[pl.ds(2 * half_here, 2), :]
        for copy in xy_copies:
            copy.start()
        sg[x] = zs[...]

    @pl.when(side == 0)
    def _():
        zs[:2, :] = keep[pl.ds(2 * z_hi, 2), :]
        sa_copy.start()
        sa[...] = zs[...]

    @pl.when(side == 1)
    def _():
        sa_copy.wait_recv()

    def turn(q):
        cols = pl.ds(pl.multiple_of(q * B, B), B)
        for l in range(2):
            inner_s[l, :, cols] = dot3(rot[l, :, cols], qg[q, l], 1, 0)

    turn(x)
    for k in (1, 3, 2):
        from_x = (x + 4 - k) % 4
        remote(qg.at[x], qg.at[from_x], s_qx.at[k - 1], r_qx.at[k - 1], partner).wait_recv()
        turn(from_x)

    for q in range(4):
        @pl.when(jnp.logical_not(jnp.logical_and(is_source, x == q)))
        def _():
            remote(zs, sg.at[q], s_xy.at[0], r_xy.at[q], partner).wait_recv()

    for l in range(2):
        left = jnp.transpose(jnp.broadcast_to(sa[l : l + 1, :], (B, B)))
        for q in range(4):
            cols = slice(q * B, (q + 1) * B)
            scaled = inner_s[l, :, cols] / (left * sg[q, l : l + 1, :] + DAMPING)
            inner_s[l, :, cols] = dot3(scaled, qg[q, l], 1, 1)
        out[l] = dot3(qa[l], inner_s[l], 1, 0).astype(out.dtype)

    for pair in one_copies:
        for copy in pair:
            copy.wait_send()
    for copy in [core_q] + core_copies + two_copies + rs_copies + ag_copies + qx_copies:
        copy.wait_send()

    @pl.when(is_source)
    def _():
        for copy in qy_copies + xy_copies:
            copy.wait_send()

    @pl.when(side == 0)
    def _():
        qa_copy.wait_send()
        sa_copy.wait_send()


def body(acts, grads_out, grad, bases_a, bases_g, owner_slot):
    rows = acts.shape[1]
    total_rows = rows * lax.axis_size("dp") * lax.axis_size("factor")
    dma = pltpu.SemaphoreType.DMA
    scratch = [
        pltpu.VMEM((4, 8, 2, 2, rows, B), acts.dtype),
        pltpu.VMEM(grad.shape, grad.dtype),
        pltpu.VMEM((2,) + bases_a.shape, F32),
        pltpu.VMEM((4, GROUP, B), F32),
        pltpu.VMEM((4, GROUP, B), F32),
        pltpu.VMEM((4, GROUP, B), F32),
        pltpu.VMEM((2, 3, SET, B), jnp.int16),
        pltpu.VMEM((2, 3, SIDE, B), F32),
        pltpu.VMEM((2, 3, SET, B), jnp.int16),
        pltpu.VMEM((2, 3, SIDE, B), F32),
        pltpu.VMEM((2, 3, B, B), F32),
        pltpu.VMEM((2, 3, 8, B), F32),
        pltpu.VMEM((2, 8, B), F32),
        pltpu.VMEM((2, 2, B, B), F32),
        pltpu.VMEM((2, B, B), F32),
        pltpu.VMEM((2, B, B), F32),
        pltpu.VMEM((3, 2, 32, B), F32),
        pltpu.VMEM((2, 32, B), F32),
        pltpu.VMEM((2, 2, B, B), F32),
        pltpu.VMEM((2, B, B), F32),
        pltpu.VMEM((4, 2, B, B), F32),
        pltpu.VMEM((8, B), F32),
        pltpu.VMEM((8, 8, B), F32),
        pltpu.VMEM((8, B), F32),
        pltpu.VMEM((4, 8, B), F32),
        pltpu.VMEM((8, B), F32),
        pltpu.VMEM((2, B, 4 * B), F32),
        pltpu.VMEM((2, B, 4 * B), F32),
        dma((7,)),
        dma((4,)), dma((4,)),
        dma((2, 3)), dma((2, 3)),
        dma((2, 3)), dma((2, 3)),
        dma((2, 3)), dma((2, 3)),
        dma((2, 3)), dma((2, 3)),
        dma, dma,
        dma((3,)), dma((3,)),
        dma((7,)), dma((7,)),
        dma((3,)), dma,
        dma((3,)), dma((3,)),
        dma((7,)), dma((7,)),
        dma((15,)), dma((4,)),
        dma((2,)), dma((2,)),
    ]
    hbm = pl.BlockSpec(memory_space=pltpu.HBM)
    return pl.pallas_call(
        functools.partial(kernel, total_rows),
        out_shape=jax.ShapeDtypeStruct(grad.shape, jnp.bfloat16),
        in_specs=[pl.BlockSpec(memory_space=pltpu.SMEM)] + [hbm] * 5,
        out_specs=pl.BlockSpec(memory_space=pltpu.VMEM),
        scratch_shapes=scratch,
        compiler_params=pltpu.CompilerParams(
            collective_id=0, has_side_effects=True, vmem_limit_bytes=63 * 1024 * 1024
        ),
        cost_estimate=pl.CostEstimate(flops=2 * 10**9, bytes_accessed=10**7, transcendentals=0),
    )(owner_slot, acts, grads_out, grad, bases_a, bases_g)


def solution(mesh):
    tokens = P(None, ("factor", "dp"), None)
    bases = P("factor", "dp", None)
    split = P(None, "dp", "factor")
    in_specs = (tokens, tokens, split, bases, bases, P())
    return jax.shard_map(body, mesh=mesh, in_specs=in_specs, out_specs=split, check_vma=False)
```

```python
import functools

import jax
import jax.numpy as jnp
from jax import lax
from jax.experimental import pallas as pl
from jax.experimental.pallas import tpu as pltpu
from jax.sharding import PartitionSpec as P

MESH = pl.DeviceIdType.MESH
B = 128
SLOTS = 2
DAMPING = 0.05
F32 = jnp.float32

GROUP = 8 * B + 8
SET = 4 * B
ORDER = (2, 1, 3, 0)
SIDE = 16
FULL = 32500.0
TINY = 1e-37


def dot(a, b, ca, cb, precision=None):
    return lax.dot_general(a, b, (((ca,), (cb,)), ((), ())), precision=precision, preferred_element_type=F32)


def halves(a):
    high = a.astype(jnp.bfloat16)
    return high, (a - high.astype(F32)).astype(jnp.bfloat16)


def dot3(a, b, ca, cb):
    (ah, al), (bh, bl) = halves(a), halves(b)
    return dot(ah, bh, ca, cb) + (dot(ah, bl, ca, cb) + dot(al, bh, ca, cb))


def kernel(total_rows, slot_ref, acts, grads, grad, bases_a, bases_g, out,
           xs, gs, bs, part, core_in, own, code, norm, in_code, in_norm, in_two, in_row, row_sum, qc, qc_in, qs, qs_in, qm, qbuf, qa, qg,
           zs, zr, sa, sg, keep, rot, inner_s,
           ld, s_core, r_core, s_one, r_one, s_norm, r_norm, s_two, r_two, s_row, r_row, s_q, r_q, s_rs, r_rs, s_ag, r_ag,
           s_qy, r_qy, s_qx, r_qx, s_z, r_z, s_xy, r_xy, s_p, r_p):
    f = lax.axis_index("factor")
    d = lax.axis_index("dp")
    z_lo, c = f // 2, f % 2
    z_hi, y, x = d // 16, (d // 4) % 4, d % 4
    z = 4 * z_hi + z_lo
    other = 1 - c
    side = 1 - (y + c) % 2
    source_row = 2 * (z_lo % 2) + c
    is_source = y == source_row
    half_here = z_lo // 2

    def at(zz, yy, xx, cc):
        return (2 * (zz % 4) + cc, 16 * (zz // 4) + 4 * yy + xx)

    def column(k):
        return (y + (k + 1) // 4) % 4, (x + (k + 1) % 4) % 4

    def block(g, m):
        if m < 4:
            return 0, m, (x + ORDER[g]) % 4
        return 1, (y + ORDER[g]) % 4, m - 4

    def along(first, k):
        return at(z, y, (x + ORDER[k]) % 4, c) if first == 0 else at(z, (y + ORDER[k]) % 4, x, c)

    def remote(src, dst, send, recv, to):
        return pltpu.make_async_remote_copy(src_ref=src, dst_ref=dst, send_sem=send, recv_sem=recv,
                                            device_id=to, device_id_type=MESH)

    partner = at(z, y, x, other)
    barrier = pltpu.get_barrier_semaphore()

    def signal(to):
        pl.semaphore_signal(barrier, inc=1, device_id=to, device_id_type=MESH)

    load_a = pltpu.make_async_copy(bases_a, bs.at[0], ld.at[4])
    load_g = pltpu.make_async_copy(bases_g, bs.at[1], ld.at[5])
    load_grad = pltpu.make_async_copy(grad, gs, ld.at[6])

    def load_group(g):
        for m in range(8):
            h, yb, xb = block(g, m)
            cols = pl.ds(pl.multiple_of((16 * h + 4 * yb + xb) * B, B), B)
            for sd, tokens in ((0, acts), (1, grads)):
                pltpu.make_async_copy(tokens.at[:, :, cols], xs.at[g, m, sd], ld.at[g]).start()

    load_a.start()
    load_g.start()
    load_group(0)

    signal(partner)
    for k in range(15):
        signal(at(z, *column(k), c))
    for k in range(1, 8):
        signal(at((z + k) % 8, y, x, c))

    load_group(1)

    load_a.wait()
    load_g.wait()
    for l in range(2):
        slot = slot_ref[l]
        mine = (slot // SLOTS) == f
        for which, sd in ((0, side), (1, 1 - side)):
            picked = jnp.where(slot % SLOTS == 0, bs[sd, 0], bs[sd, 1])
            qc[which, l] = jnp.where(mine, picked, jnp.zeros_like(picked))
    norm[...] = jnp.zeros_like(norm)
    row_sum[...] = jnp.zeros_like(row_sum)
    pl.semaphore_wait(barrier, 23)

    core_q = remote(qc.at[1], qc_in, s_q, r_q, partner)
    core_q.start()
    load_group(2)
    load_group(3)
    load_grad.start()

    iota_r = lax.broadcasted_iota(jnp.int32, (B, B), 0)
    iota_c = lax.broadcasted_iota(jnp.int32, (B, B), 1)
    iota_16 = lax.broadcasted_iota(jnp.int32, (16, B), 0)
    upper = iota_r <= iota_c
    on_diag = iota_r == iota_c

    def norms_of(tile, row0, row1):
        right = tile.astype(jnp.bfloat16)

        def outer(row):
            return dot(jnp.where(iota_16 == row, tile, 0.0).astype(jnp.bfloat16), right, 0, 0)

        return jnp.where(upper, outer(row0), outer(row1))

    def terms(core, g, dst, add):
        for m in range(8):
            yb = block(g, m)[1]
            sd = 1 - (yb + core) % 2
            x0 = xs[g, m, sd, 0]
            x1 = xs[g, m, sd, 1]
            f0 = dot(x0, x0, 0, 0)
            f1 = dot(x1, x1, 0, 0)
            packed = jnp.where(upper, f0, f1)
            diag = jnp.sum(jnp.where(on_diag, f1, 0.0), axis=0, keepdims=True)
            rows = slice(m * B, (m + 1) * B)
            row = slice(8 * B + m, 8 * B + m + 1)
            if add is not None:
                packed = packed + add[rows, :]
                diag = diag + add[row, :]
            dst[rows, :] = packed
            dst[row, :] = diag

    core_copies, one_copies = [], []

    def for_partner(g):
        pltpu.make_async_copy(xs.at[g], xs.at[g], ld.at[g]).wait()
        terms(other, g, part.at[g], None)
        copy = remote(part.at[g], core_in.at[g], s_core.at[g], r_core.at[g], partner)
        copy.start()
        core_copies.append(copy)

    def for_plane(g):
        core_copies[g].wait_recv()
        terms(c, g, own.at[g], core_in.at[g])
        if g == 3:
            for w in range(2):
                row_sum[w, 0:4, :] = own[g, 8 * B + 4 * w : 8 * B + 4 * w + 4, :]
            return
        diag0 = [jnp.sum(jnp.where(on_diag, own[g, m * B : (m + 1) * B, :], 0.0), axis=0, keepdims=True)
                 for m in range(8)]
        diag1 = own[g, 8 * B :, :]
        diag = jnp.concatenate(diag0 + [diag1], axis=0)
        inverse = jnp.where(diag > TINY, lax.rsqrt(jnp.maximum(diag, TINY)), 1.0)
        tile = inverse.astype(jnp.bfloat16).astype(F32)
        for w in range(2):
            norm[w, g, 0:4, :] = tile[4 * w : 4 * w + 4, :]
            norm[w, g, 4:8, :] = tile[8 + 4 * w : 12 + 4 * w, :]
            norm[w, g, 8:12, :] = diag1[4 * w : 4 * w + 4, :]
            for i in range(4):
                m = 4 * w + i
                unit = own[g, m * B : (m + 1) * B, :] * norms_of(tile, m, 8 + m)
                code[w, g, i * B : (i + 1) * B, :] = jnp.round(unit * FULL).astype(jnp.int32).astype(jnp.int16)
            to = along(w, g)
            pair = (remote(norm.at[w, g], in_norm.at[w, g], s_norm.at[w, g], r_norm.at[w, g], to),
                    remote(code.at[w, g], in_code.at[w, g], s_one.at[w, g], r_one.at[w, g], to))
            for copy in pair:
                copy.start()
            one_copies.append(pair)

    def decode(w, g):
        for copy in one_copies[2 * g + w]:
            copy.wait_recv()
        tile = in_norm[w, g]
        for i in range(4):
            unit = in_code[w, g, i * B : (i + 1) * B, :].astype(jnp.int32).astype(F32) * (1.0 / FULL)
            own[3, (4 * w + i) * B : (4 * w + i + 1) * B, :] += unit / norms_of(tile, i, 4 + i)
        row_sum[w, 0:4, :] += in_norm[w, g, 8:12, :]

    two_copies = []

    def second(w):
        for k in range(3):
            to = along(1 - w, k)
            u = ((y, x)[w] + ORDER[k]) % 4
            rows = pl.ds(pl.multiple_of((4 * w + u) * B, B), B)
            for copy in (remote(row_sum.at[w], in_row.at[w, k], s_row.at[w, k], r_row.at[w, k], to),
                         remote(own.at[3, rows, :], in_two.at[w, k], s_two.at[w, k], r_two.at[w, k], to)):
                copy.start()
                two_copies.append(copy)

    for_partner(0)

    core_q.wait_recv()
    for l in range(2):
        qs[l] = qc[0, l] + qc_in[l]
    rs_copies = []
    for k in range(1, 4):
        zz = (z_lo + k) % 4
        copy = remote(qs.at[:, pl.ds(pl.multiple_of(32 * zz, 32), 32), :], qs_in.at[k - 1],
                      s_rs.at[k - 1], r_rs.at[k - 1], at(4 * z_hi + zz, y, x, c))
        copy.start()
        rs_copies.append(copy)

    for_partner(1)
    for_plane(0)
    for_partner(2)
    for_plane(1)
    for_partner(3)

    for_plane(2)

    for copy in rs_copies:
        copy.wait_recv()
    here = pl.ds(pl.multiple_of(32 * z_lo, 32), 32)
    summed = qs[:, here, :] + qs_in[0] + qs_in[1] + qs_in[2]
    qm[...] = summed
    qbuf[z_hi, :, here, :] = summed
    ag_copies = []
    for k in range(1, 8):
        copy = remote(qm, qbuf.at[z_hi, :, here, :], s_ag.at[k - 1], r_ag.at[k - 1], at((z + k) % 8, y, x, c))
        copy.start()
        ag_copies.append(copy)

    for_plane(3)
    for g in range(3):
        for w in range(2):
            decode(w, g)
            if g == 2:
                second(w)

    for k in range(1, 8):
        zz = (z + 8 - k) % 8
        rows = pl.ds(pl.multiple_of(32 * (zz % 4), 32), 32)
        remote(qm, qbuf.at[zz // 4, :, rows, :], s_ag.at[k - 1], r_ag.at[k - 1], partner).wait_recv()

    qy_copies = []
    for k in range(1, 4):
        copy = remote(qbuf.at[half_here], qg.at[x], s_qy.at[k - 1], r_qy, at(z, (y + k) % 4, x, c))
        qy_copies.append(copy)
    qa_copy = remote(qbuf.at[z_hi], qa, s_p.at[0], r_p.at[0], partner)

    @pl.when(is_source)
    def _():
        for copy in qy_copies:
            copy.start()
        qg[x] = qbuf[half_here]

    @pl.when(side == 0)
    def _():
        qa_copy.start()
        qa[...] = qbuf[z_hi]

    for copy in two_copies:
        copy.wait_recv()
    zs[...] = jnp.zeros_like(zs)
    for h in range(2):
        u = 4 * h + (y, x)[h]
        packed = own[3, pl.ds(pl.multiple_of(u * B, B), B), :] + in_two[h, 0] + in_two[h, 1] + in_two[h, 2]
        row = pl.ds((y, x)[h], 1)
        diag = row_sum[h, row, :] + in_row[h, 0, row, :] + in_row[h, 1, row, :] + in_row[h, 2, row, :]
        m0 = jnp.where(upper, jnp.where(on_diag, packed, 2.0 * packed), 0.0)
        m1 = jnp.where(upper, jnp.where(on_diag, jnp.broadcast_to(diag, (B, B)), 0.0), 2.0 * packed)
        for l, m in ((0, m0), (1, m1)):
            q = qbuf[h, l]
            zs[2 * h + l : 2 * h + l + 1, :] = jnp.sum(q * dot3(m, q, 1, 0), axis=0, keepdims=True)
    z_copies = []
    for k in range(1, 8):
        copy = remote(zs, zr.at[k], s_z.at[k - 1], r_z.at[k - 1], at((z + k) % 8, y, x, c))
        copy.start()
        z_copies.append(copy)
    zr[0] = zs[...]

    @pl.when(jnp.logical_not(is_source))
    def _():
        qy_copies[0].wait_recv()

    qx_copies = []
    for k in range(1, 4):
        copy = remote(qg.at[x], qg.at[x], s_qx.at[k - 1], r_qx.at[k - 1], at(z, y, (x + k) % 4, c))
        copy.start()
        qx_copies.append(copy)

    @pl.when(side == 1)
    def _():
        qa_copy.wait_recv()

    load_grad.wait()
    for l in range(2):
        high, low = halves(qa[l])
        rot[l] = dot(high, gs[l], 0, 0) + dot(low, gs[l], 0, 0)

    for copy in z_copies:
        copy.wait_recv()
    scales = zr[0]
    for k in range(1, 8):
        scales = scales + zr[k]
    scales = scales / total_rows
    keep[...] = scales

    xy_copies = []
    for k in range(15):
        xy_copies.append(remote(zs, sg.at[x], s_xy.at[k], r_xy.at[x], at(z, *column(k), c)))
    sa_copy = remote(zs, sa, s_p.at[1], r_p.at[1], partner)

    for copy in z_copies:
        copy.wait_send()

    @pl.when(is_source)
    def _():
        zs[:2, :] = keep[pl.ds(2 * half_here, 2), :]
        for copy in xy_copies:
            copy.start()
        sg[x] = zs[...]

    @pl.when(side == 0)
    def _():
        zs[:2, :] = keep[pl.ds(2 * z_hi, 2), :]
        sa_copy.start()
        sa[...] = zs[...]

    @pl.when(side == 1)
    def _():
        sa_copy.wait_recv()

    def turn(q):
        cols = pl.ds(pl.multiple_of(q * B, B), B)
        for l in range(2):
            inner_s[l, :, cols] = dot3(rot[l, :, cols], qg[q, l], 1, 0)

    turn(x)
    for k in (1, 3, 2):
        from_x = (x + 4 - k) % 4
        remote(qg.at[x], qg.at[from_x], s_qx.at[k - 1], r_qx.at[k - 1], partner).wait_recv()
        turn(from_x)

    for q in range(4):
        @pl.when(jnp.logical_not(jnp.logical_and(is_source, x == q)))
        def _():
            remote(zs, sg.at[q], s_xy.at[0], r_xy.at[q], partner).wait_recv()

    for l in range(2):
        left = jnp.transpose(jnp.broadcast_to(sa[l : l + 1, :], (B, B)))
        for q in range(4):
            cols = slice(q * B, (q + 1) * B)
            scaled = inner_s[l, :, cols] / (left * sg[q, l : l + 1, :] + DAMPING)
            inner_s[l, :, cols] = dot3(scaled, qg[q, l], 1, 1)
        out[l] = dot3(qa[l], inner_s[l], 1, 0).astype(out.dtype)

    for pair in one_copies:
        for copy in pair:
            copy.wait_send()
    for copy in [core_q] + core_copies + two_copies + rs_copies + ag_copies + qx_copies:
        copy.wait_send()

    @pl.when(is_source)
    def _():
        for copy in qy_copies + xy_copies:
            copy.wait_send()

    @pl.when(side == 0)
    def _():
        qa_copy.wait_send()
        sa_copy.wait_send()


def body(acts, grads_out, grad, bases_a, bases_g, owner_slot):
    rows = acts.shape[1]
    total_rows = rows * lax.axis_size("dp") * lax.axis_size("factor")
    dma = pltpu.SemaphoreType.DMA
    scratch = [
        pltpu.VMEM((4, 8, 2, 2, rows, B), acts.dtype),
        pltpu.VMEM(grad.shape, grad.dtype),
        pltpu.VMEM((2,) + bases_a.shape, F32),
        pltpu.VMEM((4, GROUP, B), F32),
        pltpu.VMEM((4, GROUP, B), F32),
        pltpu.VMEM((4, GROUP, B), F32),
        pltpu.VMEM((2, 3, SET, B), jnp.int16),
        pltpu.VMEM((2, 3, SIDE, B), F32),
        pltpu.VMEM((2, 3, SET, B), jnp.int16),
        pltpu.VMEM((2, 3, SIDE, B), F32),
        pltpu.VMEM((2, 3, B, B), F32),
        pltpu.VMEM((2, 3, 8, B), F32),
        pltpu.VMEM((2, 8, B), F32),
        pltpu.VMEM((2, 2, B, B), F32),
        pltpu.VMEM((2, B, B), F32),
        pltpu.VMEM((2, B, B), F32),
        pltpu.VMEM((3, 2, 32, B), F32),
        pltpu.VMEM((2, 32, B), F32),
        pltpu.VMEM((2, 2, B, B), F32),
        pltpu.VMEM((2, B, B), F32),
        pltpu.VMEM((4, 2, B, B), F32),
        pltpu.VMEM((8, B), F32),
        pltpu.VMEM((8, 8, B), F32),
        pltpu.VMEM((8, B), F32),
        pltpu.VMEM((4, 8, B), F32),
        pltpu.VMEM((8, B), F32),
        pltpu.VMEM((2, B, 4 * B), F32),
        pltpu.VMEM((2, B, 4 * B), F32),
        dma((7,)),
        dma((4,)), dma((4,)),
        dma((2, 3)), dma((2, 3)),
        dma((2, 3)), dma((2, 3)),
        dma((2, 3)), dma((2, 3)),
        dma((2, 3)), dma((2, 3)),
        dma, dma,
        dma((3,)), dma((3,)),
        dma((7,)), dma((7,)),
        dma((3,)), dma,
        dma((3,)), dma((3,)),
        dma((7,)), dma((7,)),
        dma((15,)), dma((4,)),
        dma((2,)), dma((2,)),
    ]
    hbm = pl.BlockSpec(memory_space=pltpu.HBM)
    return pl.pallas_call(
        functools.partial(kernel, total_rows),
        out_shape=jax.ShapeDtypeStruct(grad.shape, jnp.bfloat16),
        in_specs=[pl.BlockSpec(memory_space=pltpu.SMEM)] + [hbm] * 5,
        out_specs=pl.BlockSpec(memory_space=pltpu.VMEM),
        scratch_shapes=scratch,
        compiler_params=pltpu.CompilerParams(
            collective_id=0, has_side_effects=True, vmem_limit_bytes=63 * 1024 * 1024
        ),
        cost_estimate=pl.CostEstimate(flops=2 * 10**9, bytes_accessed=10**7, transcendentals=0),
    )(owner_slot, acts, grads_out, grad, bases_a, bases_g)


def solution(mesh):
    tokens = P(None, ("factor", "dp"), None)
    bases = P("factor", "dp", None)
    split = P(None, "dp", "factor")
    in_specs = (tokens, tokens, split, bases, bases, P())
    return jax.shard_map(body, mesh=mesh, in_specs=in_specs, out_specs=split, check_vma=False)
```
